32 devices in a mesh: freq: 4 (over z), rcv: 8 (over y, x, core).
Axes of the slice: x: 2, y: 2, z: 4, core: 2. Of those that a mesh axis runs over, the one named last changes fastest.
Arguments:
- reflection: float32 [128, 2, 1024, 2048], P('freq', None, None, 'rcv'), may hold values from -0.09375 to 0.09375
- focusing_input: float32 [128, 2, 32, 2048], P('freq', None, None, 'rcv'), may hold values from -6 to 6
- direct_wave: float32 [256, 32, 2048], P(None, 'freq', 'rcv'), may hold values from -6 to 6
- mute_source: int32 [32, 1024], P('rcv', 'freq'), may hold values from 32 to 127
- mute_receiver: int32 [32, 2048], P('freq', 'rcv'), may hold values from 32 to 127
Outputs:
- focus_minus: float32 [256, 32, 1024], P(None, 'rcv', 'freq')
- focus_plus: float32 [256, 32, 2048], P(None, 'freq', 'rcv')
The draws below stay inside these ranges and needn't reach their ends.
All inputs are finite; a program needn't handle non-finite values.
Results may differ from the reference program's by a relative error of at most 0.00007.
Values sent between devices are 32-bit elements; how exact they have to be, the bound alone decides.
A program may use at most 192 MiB of HBM per device.

```python
import math
import jax
import jax.numpy as jnp
from jax import lax

F = 128
S = 1024
RCV = 2048
P_SIZE = 32
NT = 256


def set_ends(array, rng, least, top_value):
    longest = array.shape.index(max(array.shape))
    spots = []
    for shift in (0, 1):
        where = [jax.random.randint(jax.random.fold_in(rng, axis), (), 0, length) for axis, length in enumerate(array.shape)]
        where[longest] = (where[longest] + shift) % array.shape[longest]
        spots.append(tuple(where))
    return array.at[spots[0]].set(least).at[spots[1]].set(top_value)


def block_scale(own_key, shape, pieces, smallest, top_value):
    gain, own = 1.0, jax.random.fold_in(own_key, 6)
    for position, blocks in pieces:
        heights = jnp.exp(jax.random.uniform(jax.random.fold_in(own, position), (blocks,), jnp.float32, smallest / len(pieces), top_value / len(pieces)))
        gain = gain * jnp.repeat(heights, shape[position] // blocks).reshape([-1 if axis == position else 1 for axis in range(len(shape))])
    return gain


def gaussian(key, dims, width, limit, cuts=(), kind=jnp.bfloat16):
    loudness = block_scale(key, dims, cuts, -0.22, 0.18) if cuts else 1.0
    values = jax.random.normal(key, dims, jnp.float32) * width * loudness
    return jnp.minimum(jnp.maximum(values, -limit), limit).astype(kind)


def setup_inputs(seed: int = 0) -> dict:
    key_of = jax.random.split(jax.random.key(seed), 6)
    reflection = gaussian(key_of[0], (F, 2, S, RCV), (2 * RCV) ** -0.5, 0.09375, ((0, 4), (3, 8)), jnp.float32)
    focusing_input = gaussian(key_of[1], (F, 2, P_SIZE, RCV), 1.0, 6.0, ((0, 4), (3, 8)), jnp.float32)
    direct_wave = gaussian(key_of[2], (NT, P_SIZE, RCV), 1.0, 6.0, ((1, 4), (2, 8)), jnp.float32)
    mute_source = set_ends(jax.random.randint(key_of[3], (P_SIZE, S), NT // 8, NT // 2), jax.random.fold_in(key_of[3], 1), NT // 8, (NT // 2) - 1).astype(jnp.int32)
    mute_receiver = set_ends(jax.random.randint(key_of[4], (P_SIZE, RCV), NT // 8, NT // 2), jax.random.fold_in(key_of[4], 1), NT // 8, (NT // 2) - 1).astype(jnp.int32)
    return dict(reflection=reflection, focusing_input=focusing_input, direct_wave=direct_wave, mute_source=mute_source, mute_receiver=mute_receiver)


MAXIMUM_ACCURACY = lax.Precision.HIGHEST

def dft_tables():
    index_freq = jnp.arange(F, dtype=jnp.int32)[:, None] + 1
    index_time = jnp.arange(NT, dtype=jnp.int32)[None, :]
    phase_turns = jnp.mod(index_freq * index_time, NT).astype(jnp.float32) * (2.0 * math.pi / NT)
    return (jnp.cos(phase_turns), jnp.sin(phase_turns))

def window(traces, mute_table):
    time_index = jnp.arange(NT, dtype=jnp.int32)[:, None, None]
    kept_mask = (time_index < mute_table[None]) | (time_index > NT - mute_table[None])
    return jnp.where(kept_mask, traces, jnp.zeros_like(traces))

def reference(reflection, focusing_input, direct_wave, mute_source, mute_receiver):
    cosine, sine_table = dft_tables()
    factor = 1.0 / math.sqrt(F)
    reflection_real = reflection[:, 0]
    reflection_imaginary = reflection[:, 1]
    focusing_real = focusing_input[:, 0]
    focusing_imaginary = focusing_input[:, 1]
    upgoing_real = jnp.einsum('ual,uel->eua', reflection_real, focusing_real, precision=MAXIMUM_ACCURACY) - jnp.einsum('ual,uel->eua', reflection_imaginary, focusing_imaginary, precision=MAXIMUM_ACCURACY)
    upgoing_imaginary = jnp.einsum('ual,uel->eua', reflection_real, focusing_imaginary, precision=MAXIMUM_ACCURACY) + jnp.einsum('ual,uel->eua', reflection_imaginary, focusing_real, precision=MAXIMUM_ACCURACY)
    up_time = factor * (jnp.einsum('pfs,ft->tps', upgoing_real, cosine, precision=MAXIMUM_ACCURACY) - jnp.einsum('pfs,ft->tps', upgoing_imaginary, sine_table, precision=MAXIMUM_ACCURACY))
    focus_minus = window(up_time, mute_source)
    backward_real = factor * jnp.einsum('tps,ft->pfs', focus_minus, cosine, precision=MAXIMUM_ACCURACY)
    backward_imaginary = -factor * jnp.einsum('tps,ft->pfs', focus_minus, sine_table, precision=MAXIMUM_ACCURACY)
    adjoint_real_values = jnp.einsum('klh,lhc->klc', backward_real, reflection_real, precision=MAXIMUM_ACCURACY) + jnp.einsum('klh,lhc->klc', backward_imaginary, reflection_imaginary, precision=MAXIMUM_ACCURACY)
    adjoint_imaginary = jnp.einsum('klh,lhc->klc', backward_imaginary, reflection_real, precision=MAXIMUM_ACCURACY) - jnp.einsum('klh,lhc->klc', backward_real, reflection_imaginary, precision=MAXIMUM_ACCURACY)
    adj_time = factor * (jnp.einsum('pfr,ft->tpr', adjoint_real_values, cosine, precision=MAXIMUM_ACCURACY) - jnp.einsum('pfr,ft->tpr', adjoint_imaginary, sine_table, precision=MAXIMUM_ACCURACY))
    focus_plus = direct_wave - window(adj_time, mute_receiver)
    return (focus_minus, focus_plus)
```

```python
import functools
import math

import jax
import jax.numpy as jnp
import ml_dtypes
import numpy as np
from jax import lax
from jax.experimental import pallas as pl
from jax.experimental.pallas import tpu as pltpu
from jax.sharding import PartitionSpec as P

LIMIT = 40 * 1024 * 1024
LANES = 128


def split(value):
    high = value.astype(jnp.bfloat16)
    low = (value - high.astype(jnp.float32)).astype(jnp.bfloat16)
    return high, low


def dot(a, b):
    return jnp.dot(a, b, preferred_element_type=jnp.float32)


def dot_nt(a, b):
    return lax.dot_general(a, b, (((1,), (1,)), ((), ())), preferred_element_type=jnp.float32)


def left3(stacked, high, matrix, product):
    rows = high.shape[0]
    matrix_high, matrix_low = split(matrix)
    both = product(stacked, matrix_high)
    return both[:rows] + both[rows:] + product(high, matrix_low)


def table3(table_high, table_low, value):
    value_high, value_low = split(value)
    return dot(table_high, value_high) + dot(table_low, value_high) + dot(table_high, value_low)


def turned(value, share, sign):
    rows = value.shape[0]
    row = lax.broadcasted_iota(jnp.int32, value.shape, 0)
    is_real = row % (2 * share) < share
    from_imag = pltpu.roll(value, rows - share, 0)
    from_real = pltpu.roll(value, share, 0)
    return jnp.where(is_real, -sign * from_imag, sign * from_real)


def forward_kernel(share, refl_ref, focus_ref, out_ref):
    groups, parts, steps, rows, width = out_ref.shape
    for step in range(steps):
        high, low = split(focus_ref[step])
        stacked = jnp.concatenate([high, low], axis=0)
        real, imag = (
            left3(stacked, high, refl_ref[step, c].reshape(parts * width, -1), dot_nt)
            for c in (0, 1)
        )
        panel = real + turned(imag, share, 1.0)
        for part in range(parts):
            out_ref[:, part, step] = panel[:, part * width : (part + 1) * width].reshape(
                groups, rows, width
            )


def forward(refl, focus, chunk, width, groups, share):
    freqs, _, parts, _, receivers = refl.shape
    steps = 2
    return pl.pallas_call(
        functools.partial(forward_kernel, share),
        grid=(freqs // steps,),
        in_specs=[
            pl.BlockSpec((steps, 2, parts, width, receivers), lambda k: (k, 0, 0, chunk, 0)),
            pl.BlockSpec((steps, groups * 2 * share, receivers), lambda k: (k, 0, 0)),
        ],
        out_specs=pl.BlockSpec(
            (groups, parts, steps, 2 * share, width), lambda k: (0, 0, k, 0, 0)
        ),
        out_shape=jax.ShapeDtypeStruct(
            (groups, parts, freqs, 2 * share, width), jnp.float32
        ),
        compiler_params=pltpu.CompilerParams(vmem_limit_bytes=LIMIT),
        cost_estimate=pl.CostEstimate(
            flops=6 * 2 * freqs * 2 * parts * width * receivers * groups * 2 * share,
            bytes_accessed=4 * freqs * 2 * parts * width * (receivers + groups * share),
            transcendentals=0,
        ),
        name="forward",
    )(refl, focus)


def adjoint_kernel(share, refl_ref, spec_ref, *rest):
    prev_ref, out_ref = rest if len(rest) == 2 else (None, rest[0])
    groups, parts, steps, rows, width = spec_ref.shape
    for step in range(steps):
        spec = jnp.concatenate(
            [spec_ref[:, part, step].reshape(groups * rows, width) for part in range(parts)],
            axis=1,
        )
        high, low = split(spec)
        stacked = jnp.concatenate([high, low], axis=0)
        real, imag = (
            left3(stacked, high, refl_ref[step, c].reshape(parts * width, -1), dot)
            for c in (0, 1)
        )
        panel = (real + turned(imag, share, -1.0)).reshape(out_ref[:, step].shape)
        if prev_ref is not None:
            panel = panel + prev_ref[:, step]
        out_ref[:, step] = panel


def adjoint(refl, spec, prev, chunk, width, groups, share):
    freqs, _, parts, _, receivers = refl.shape
    steps = 2
    shape = (parts, freqs, groups // parts, 2 * share, receivers)
    out_spec = pl.BlockSpec(
        (parts, steps, groups // parts, 2 * share, receivers), lambda k: (0, k, 0, 0, 0)
    )
    more = [] if prev is None else [prev]
    return pl.pallas_call(
        functools.partial(adjoint_kernel, share),
        grid=(freqs // steps,),
        in_specs=[
            pl.BlockSpec((steps, 2, parts, width, receivers), lambda k: (k, 0, 0, chunk, 0)),
            pl.BlockSpec(
                (groups, parts, steps, 2 * share, width), lambda k: (0, 0, k, 0, 0)
            ),
        ]
        + [out_spec] * len(more),
        out_specs=out_spec,
        out_shape=jax.ShapeDtypeStruct(shape, jnp.float32),
        compiler_params=pltpu.CompilerParams(vmem_limit_bytes=LIMIT),
        cost_estimate=pl.CostEstimate(
            flops=6 * 2 * freqs * 2 * parts * width * receivers * groups * 2 * share,
            bytes_accessed=4 * freqs * 2 * parts * width * (receivers + groups * share),
            transcendentals=0,
        ),
        name="adjoint",
    )(refl, spec, *more)


def kept(samples, mute, width):
    time = lax.broadcasted_iota(jnp.int32, (samples, width), 0)
    return (time < mute) | (time > samples - mute)


def window_kernel(share, to_time, to_freq, mute_ref, spec_ref, *rest):
    trace_ref, back_ref = rest[-2:]
    freqs, _, width = spec_ref.shape
    samples = 2 * freqs
    for point in range(share):
        spec = jnp.concatenate([spec_ref[:, point, :], spec_ref[:, share + point, :]], axis=0)
        trace = table3(to_time[0], to_time[1], spec)
        trace = jnp.where(kept(samples, mute_ref[point : point + 1, :], width), trace, 0.0)
        trace_ref[:, point, :] = trace
        back = table3(to_freq[0], to_freq[1], trace)
        back_ref[:, point, :] = back[:freqs]
        back_ref[:, share + point, :] = back[freqs:]


def window_source(to_time, to_freq, mute, spec, traces, chunk, width, share):
    freqs = spec.shape[0]
    samples = 2 * freqs
    more = [] if traces is None else [traces]
    whole = lambda k: (0, 0, 0)
    return pl.pallas_call(
        functools.partial(window_kernel, share),
        grid=(1,),
        in_specs=[
            pl.BlockSpec(to_time.shape, whole),
            pl.BlockSpec(to_freq.shape, whole),
            pl.BlockSpec((share, width), lambda k: (0, chunk)),
            pl.BlockSpec(spec.shape, whole),
        ]
        + [pl.BlockSpec(memory_space=pl.ANY)] * len(more),
        out_specs=[
            pl.BlockSpec((samples, share, width), lambda k: (0, 0, chunk)),
            pl.BlockSpec(spec.shape, whole),
        ],
        out_shape=[
            jax.ShapeDtypeStruct((samples, share, mute.shape[1]), jnp.float32),
            jax.ShapeDtypeStruct(spec.shape, jnp.float32),
        ],
        input_output_aliases={4: 0} if more else {},
        compiler_params=pltpu.CompilerParams(vmem_limit_bytes=LIMIT),
        cost_estimate=pl.CostEstimate(
            flops=3 * 4 * samples * samples * share * width,
            bytes_accessed=4 * 3 * samples * share * width,
            transcendentals=0,
        ),
        name="window_source",
    )(to_time, to_freq, mute, spec, *more)


def final_kernel(share, to_time, mute_ref, spec_ref, direct_ref, out_ref):
    freqs, _, width = spec_ref.shape
    samples = 2 * freqs
    for point in range(out_ref.shape[1]):
        row = point // share * 2 * share + point % share
        spec = jnp.concatenate([spec_ref[:, row, :], spec_ref[:, row + share, :]], axis=0)
        trace = table3(to_time[0], to_time[1], spec)
        trace = jnp.where(kept(samples, mute_ref[point : point + 1, :], width), trace, 0.0)
        out_ref[:, point, :] = direct_ref[:, point, :] - trace


def final(to_time, mute, spec, direct, share):
    samples, points, receivers = direct.shape
    freqs, rows, _ = spec.shape
    width = min(LANES, receivers)
    return pl.pallas_call(
        functools.partial(final_kernel, share),
        grid=(receivers // width,),
        in_specs=[
            pl.BlockSpec(to_time.shape, lambda k: (0, 0, 0)),
            pl.BlockSpec((points, width), lambda k: (0, k)),
            pl.BlockSpec((freqs, rows, width), lambda k: (0, 0, k)),
            pl.BlockSpec((samples, points, width), lambda k: (0, 0, k)),
        ],
        out_specs=pl.BlockSpec((samples, points, width), lambda k: (0, 0, k)),
        out_shape=jax.ShapeDtypeStruct(direct.shape, jnp.float32),
        compiler_params=pltpu.CompilerParams(vmem_limit_bytes=LIMIT),
        cost_estimate=pl.CostEstimate(
            flops=3 * 2 * samples * samples * points * receivers,
            bytes_accessed=4 * 3 * samples * points * receivers,
            transcendentals=0,
        ),
        name="final",
    )(to_time, mute, spec, direct)


def tables(freqs):
    samples = 2 * freqs
    turns = (np.arange(1, freqs + 1)[:, None] * np.arange(samples)[None, :]) % samples
    phase = turns * (2.0 * np.pi / samples)
    whole = np.concatenate([np.cos(phase), -np.sin(phase)], axis=0) / math.sqrt(freqs)
    high = whole.astype(ml_dtypes.bfloat16)
    low = (whole - high.astype(np.float64)).astype(ml_dtypes.bfloat16)
    both = np.stack([high, low])
    return jnp.asarray(np.ascontiguousarray(both.transpose(0, 2, 1))), jnp.asarray(both)


def body(reflection, focusing_input, direct_wave, mute_source, mute_receiver):
    freq_devices = lax.axis_size("freq")
    groups = lax.axis_size("rcv")
    local, _, sources, receivers = reflection.shape
    freqs = local * freq_devices
    share, own = mute_source.shape
    points = share * groups
    width = min(LANES, own)
    chunks = own // width
    to_time, to_freq = tables(freqs)
    refl = reflection.reshape(local, 2, freq_devices, own, receivers)
    focus = focusing_input.reshape(local, 2, groups, share, receivers)
    focus = focus.transpose(0, 2, 1, 3, 4).reshape(local, 2 * points, receivers)

    specs = []
    for chunk in range(chunks):
        term = forward(refl, focus, chunk, width, groups, share)
        summed = lax.psum_scatter(term, "rcv", scatter_dimension=0, tiled=False)
        spec = lax.all_to_all(summed, "freq", split_axis=0, concat_axis=0, tiled=True)
        specs.append(spec.reshape(freqs, 2 * share, width))
    traces = None
    gathered = []
    for chunk in range(chunks):
        traces, back = window_source(
            to_time, to_freq, mute_source, specs[chunk], traces, chunk, width, share
        )
        back = back.reshape(freq_devices, local, 2 * share, width)
        back = lax.all_to_all(back, "freq", split_axis=0, concat_axis=0, tiled=True)
        gathered.append(lax.all_gather(back, "rcv", axis=0, tiled=False))
    panel = None
    for chunk in range(chunks):
        panel = adjoint(refl, gathered[chunk], panel, chunk, width, groups, share)
    panel = lax.all_to_all(panel, "freq", split_axis=0, concat_axis=0, tiled=True)
    panel = panel.reshape(freqs, groups // freq_devices * 2 * share, receivers)
    return traces, final(to_time, mute_receiver, panel, direct_wave, share)


def solution(mesh):
    placed = (
        P("freq", None, None, "rcv"),
        P("freq", None, None, "rcv"),
        P(None, "freq", "rcv"),
        P("rcv", "freq"),
        P("freq", "rcv"),
    )
    return jax.shard_map(
        body,
        mesh=mesh,
        in_specs=placed,
        out_specs=(P(None, "rcv", "freq"), P(None, "freq", "rcv")),
        check_vma=False,
    )
```

```python
import functools
import math

import jax
import jax.numpy as jnp
import ml_dtypes
import numpy as np
from jax import lax
from jax.experimental import pallas as pl
from jax.experimental.pallas import tpu as pltpu
from jax.sharding import PartitionSpec as P

LIMIT = 40 * 1024 * 1024
LANES = 128


def split(value):
    high = value.astype(jnp.bfloat16)
    low = (value - high.astype(jnp.float32)).astype(jnp.bfloat16)
    return high, low


def dot(a, b):
    return jnp.dot(a, b, preferred_element_type=jnp.float32)


def dot_nt(a, b):
    return lax.dot_general(a, b, (((1,), (1,)), ((), ())), preferred_element_type=jnp.float32)


def left3(stacked, high, matrix, product):
    rows = high.shape[0]
    matrix_high, matrix_low = split(matrix)
    both = product(stacked, matrix_high)
    return both[:rows] + both[rows:] + product(high, matrix_low)


def table3(table_high, table_low, value):
    value_high, value_low = split(value)
    return dot(table_high, value_high) + dot(table_low, value_high) + dot(table_high, value_low)


def turned(value, share, sign):
    rows = value.shape[0]
    row = lax.broadcasted_iota(jnp.int32, value.shape, 0)
    is_real = row % (2 * share) < share
    from_imag = pltpu.roll(value, rows - share, 0)
    from_real = pltpu.roll(value, share, 0)
    return jnp.where(is_real, -sign * from_imag, sign * from_real)


def forward_kernel(share, me_ref, refl_ref, focus_ref, keep_ref, send_ref):
    half, parts, steps, rows, width = keep_ref.shape
    groups = 2 * half
    order = [*range(0, groups, 2), *range(1, groups, 2)]
    for step in range(steps):
        focus = jnp.concatenate([focus_ref[step, g ^ me_ref[0]] for g in order], axis=0)
        high, low = split(focus)
        stacked = jnp.concatenate([high, low], axis=0)
        real, imag = (
            left3(stacked, high, refl_ref[step, c].reshape(parts * width, -1), dot_nt)
            for c in (0, 1)
        )
        panel = real + turned(imag, share, 1.0)
        for part in range(parts):
            block = panel[:, part * width : (part + 1) * width].reshape(groups, rows, width)
            keep_ref[:, part, step] = block[:half]
            send_ref[:, part, step] = block[half:]


def forward(me, refl, focus, chunk, width, groups, share):
    freqs, _, parts, _, receivers = refl.shape
    steps = 2
    return pl.pallas_call(
        functools.partial(forward_kernel, share),
        grid=(freqs // steps,),
        in_specs=[
            pl.BlockSpec(memory_space=pltpu.SMEM),
            pl.BlockSpec((steps, 2, parts, width, receivers), lambda k: (k, 0, 0, chunk, 0)),
            pl.BlockSpec((steps, groups, 2 * share, receivers), lambda k: (k, 0, 0, 0)),
        ],
        out_specs=[
            pl.BlockSpec((groups // 2, parts, steps, 2 * share, width), lambda k: (0, 0, k, 0, 0))
        ]
        * 2,
        out_shape=[
            jax.ShapeDtypeStruct((groups // 2, parts, freqs, 2 * share, width), jnp.float32)
        ]
        * 2,
        compiler_params=pltpu.CompilerParams(vmem_limit_bytes=LIMIT),
        cost_estimate=pl.CostEstimate(
            flops=6 * 2 * freqs * 2 * parts * width * receivers * groups * 2 * share,
            bytes_accessed=4 * freqs * 2 * parts * width * (receivers + groups * share),
            transcendentals=0,
        ),
        name="forward",
    )(me, refl, focus)


def adjoint_kernel(share, me_ref, refl_ref, own_ref, other_ref, *rest):
    prev_ref, out_ref = rest if len(rest) == 2 else (None, rest[0])
    half, parts, steps, rows, width = own_ref.shape
    odd = me_ref[0] % 2 == 1
    pair = me_ref[0] // 2
    for step in range(steps):
        columns = []
        for part in range(parts):
            pieces = []
            for g in range(half):
                own = own_ref[g ^ pair, part, step]
                other = other_ref[g ^ pair, part, step]
                pieces += [jnp.where(odd, other, own), jnp.where(odd, own, other)]
            columns.append(jnp.concatenate(pieces, axis=0))
        spec = jnp.concatenate(columns, axis=1)
        high, low = split(spec)
        stacked = jnp.concatenate([high, low], axis=0)
        real, imag = (
            left3(stacked, high, refl_ref[step, c].reshape(parts * width, -1), dot)
            for c in (0, 1)
        )
        panel = (real + turned(imag, share, -1.0)).reshape(out_ref[:, step].shape)
        if prev_ref is not None:
            panel = panel + prev_ref[:, step]
        out_ref[:, step] = panel


def adjoint(me, refl, own, other, prev, chunk, width, groups, share):
    freqs, _, parts, _, receivers = refl.shape
    steps = 2
    shape = (parts, freqs, groups // parts, 2 * share, receivers)
    out_spec = pl.BlockSpec(
        (parts, steps, groups // parts, 2 * share, receivers), lambda k: (0, k, 0, 0, 0)
    )
    more = [] if prev is None else [prev]
    return pl.pallas_call(
        functools.partial(adjoint_kernel, share),
        grid=(freqs // steps,),
        in_specs=[
            pl.BlockSpec(memory_space=pltpu.SMEM),
            pl.BlockSpec((steps, 2, parts, width, receivers), lambda k: (k, 0, 0, chunk, 0)),
        ]
        + [
            pl.BlockSpec((groups // 2, parts, steps, 2 * share, width), lambda k: (0, 0, k, 0, 0))
        ]
        * 2
        + [out_spec] * len(more),
        out_specs=out_spec,
        out_shape=jax.ShapeDtypeStruct(shape, jnp.float32),
        compiler_params=pltpu.CompilerParams(vmem_limit_bytes=LIMIT),
        cost_estimate=pl.CostEstimate(
            flops=6 * 2 * freqs * 2 * parts * width * receivers * groups * 2 * share,
            bytes_accessed=4 * freqs * 2 * parts * width * (receivers + groups * share),
            transcendentals=0,
        ),
        name="adjoint",
    )(me, refl, own, other, *more)


def kept(samples, mute, width):
    time = lax.broadcasted_iota(jnp.int32, (samples, width), 0)
    return (time < mute) | (time > samples - mute)


def window_kernel(share, to_time, to_freq, mute_ref, spec_ref, *rest):
    trace_ref, back_ref = rest[-2:]
    freqs, _, width = spec_ref.shape
    samples = 2 * freqs
    for point in range(share):
        spec = jnp.concatenate([spec_ref[:, point, :], spec_ref[:, share + point, :]], axis=0)
        trace = table3(to_time[0], to_time[1], spec)
        trace = jnp.where(kept(samples, mute_ref[point : point + 1, :], width), trace, 0.0)
        trace_ref[:, point, :] = trace
        back = table3(to_freq[0], to_freq[1], trace)
        back_ref[:, point, :] = back[:freqs]
        back_ref[:, share + point, :] = back[freqs:]


def window_source(to_time, to_freq, mute, spec, traces, chunk, width, share):
    freqs = spec.shape[0]
    samples = 2 * freqs
    more = [] if traces is None else [traces]
    whole = lambda k: (0, 0, 0)
    return pl.pallas_call(
        functools.partial(window_kernel, share),
        grid=(1,),
        in_specs=[
            pl.BlockSpec(to_time.shape, whole),
            pl.BlockSpec(to_freq.shape, whole),
            pl.BlockSpec((share, width), lambda k: (0, chunk)),
            pl.BlockSpec(spec.shape, whole),
        ]
        + [pl.BlockSpec(memory_space=pl.ANY)] * len(more),
        out_specs=[
            pl.BlockSpec((samples, share, width), lambda k: (0, 0, chunk)),
            pl.BlockSpec(spec.shape, whole),
        ],
        out_shape=[
            jax.ShapeDtypeStruct((samples, share, mute.shape[1]), jnp.float32),
            jax.ShapeDtypeStruct(spec.shape, jnp.float32),
        ],
        input_output_aliases={4: 0} if more else {},
        compiler_params=pltpu.CompilerParams(vmem_limit_bytes=LIMIT),
        cost_estimate=pl.CostEstimate(
            flops=3 * 4 * samples * samples * share * width,
            bytes_accessed=4 * 3 * samples * share * width,
            transcendentals=0,
        ),
        name="window_source",
    )(to_time, to_freq, mute, spec, *more)


def final_kernel(share, to_time, mute_ref, spec_ref, direct_ref, out_ref):
    freqs, _, width = spec_ref.shape
    samples = 2 * freqs
    for point in range(out_ref.shape[1]):
        row = point // share * 2 * share + point % share
        spec = jnp.concatenate([spec_ref[:, row, :], spec_ref[:, row + share, :]], axis=0)
        trace = table3(to_time[0], to_time[1], spec)
        trace = jnp.where(kept(samples, mute_ref[point : point + 1, :], width), trace, 0.0)
        out_ref[:, point, :] = direct_ref[:, point, :] - trace


def final(to_time, mute, spec, direct, share):
    samples, points, receivers = direct.shape
    freqs, rows, _ = spec.shape
    width = min(LANES, receivers)
    return pl.pallas_call(
        functools.partial(final_kernel, share),
        grid=(receivers // width,),
        in_specs=[
            pl.BlockSpec(to_time.shape, lambda k: (0, 0, 0)),
            pl.BlockSpec((points, width), lambda k: (0, k)),
            pl.BlockSpec((freqs, rows, width), lambda k: (0, 0, k)),
            pl.BlockSpec((samples, points, width), lambda k: (0, 0, k)),
        ],
        out_specs=pl.BlockSpec((samples, points, width), lambda k: (0, 0, k)),
        out_shape=jax.ShapeDtypeStruct(direct.shape, jnp.float32),
        compiler_params=pltpu.CompilerParams(vmem_limit_bytes=LIMIT),
        cost_estimate=pl.CostEstimate(
            flops=3 * 2 * samples * samples * points * receivers,
            bytes_accessed=4 * 3 * samples * points * receivers,
            transcendentals=0,
        ),
        name="final",
    )(to_time, mute, spec, direct)


def tables(freqs):
    samples = 2 * freqs
    turns = (np.arange(1, freqs + 1)[:, None] * np.arange(samples)[None, :]) % samples
    phase = turns * (2.0 * np.pi / samples)
    whole = np.concatenate([np.cos(phase), -np.sin(phase)], axis=0) / math.sqrt(freqs)
    high = whole.astype(ml_dtypes.bfloat16)
    low = (whole - high.astype(np.float64)).astype(ml_dtypes.bfloat16)
    both = np.stack([high, low])
    return jnp.asarray(np.ascontiguousarray(both.transpose(0, 2, 1))), jnp.asarray(both)


def swap(value, groups, bit):
    return lax.ppermute(value, "rcv", [(i, i ^ (1 << bit)) for i in range(groups)])


def scatter_half(value, groups, bits):
    rest = list(bits)
    while rest:
        bit = rest.pop(0)
        axis = sum(b > bit for b in rest)
        mine = lax.index_in_dim(value, 0, axis, keepdims=False)
        value = mine + swap(lax.index_in_dim(value, 1, axis, keepdims=False), groups, bit)
    return value


def gather_half(value, groups, bits):
    done = []
    for bit in bits:
        axis = sum(b > bit for b in done)
        value = jnp.stack([value, swap(value, groups, bit)], axis=axis)
        done.append(bit)
    return value


def scatter(keep, send, groups):
    total = keep + swap(send, groups, 0)
    bits = list(range(1, groups.bit_length() - 1))
    total = total.reshape((2,) * len(bits) + keep.shape[1:])
    cut = keep.shape[2] // 2
    axis = len(bits) + 1
    first = scatter_half(lax.slice_in_dim(total, 0, cut, axis=axis), groups, bits)
    second = scatter_half(lax.slice_in_dim(total, cut, None, axis=axis), groups, bits[::-1])
    return jnp.concatenate([first, second], axis=1)


def gather(value, groups):
    bits = list(range(1, groups.bit_length() - 1))
    cut = value.shape[1] // 2
    first = gather_half(value[:, :cut], groups, bits)
    second = gather_half(value[:, cut:], groups, bits[::-1])
    own = jnp.concatenate([first, second], axis=len(bits) + 1)
    own = own.reshape((groups // 2,) + value.shape)
    return own, swap(own, groups, 0)


def body(reflection, focusing_input, direct_wave, mute_source, mute_receiver):
    freq_devices = lax.axis_size("freq")
    groups = lax.axis_size("rcv")
    local, _, sources, receivers = reflection.shape
    freqs = local * freq_devices
    share, own = mute_source.shape
    width = min(LANES, own)
    chunks = own // width
    to_time, to_freq = tables(freqs)
    refl = reflection.reshape(local, 2, freq_devices, own, receivers)
    focus = focusing_input.reshape(local, 2, groups, share, receivers)
    focus = focus.transpose(0, 2, 1, 3, 4).reshape(local, groups, 2 * share, receivers)
    me = lax.axis_index("rcv").astype(jnp.int32).reshape(1)

    specs = []
    for chunk in range(chunks):
        keep, send = forward(me, refl, focus, chunk, width, groups, share)
        summed = scatter(keep, send, groups)
        spec = lax.all_to_all(summed, "freq", split_axis=0, concat_axis=0, tiled=True)
        specs.append(spec.reshape(freqs, 2 * share, width))
    traces = None
    gathered = []
    for chunk in range(chunks):
        traces, back = window_source(
            to_time, to_freq, mute_source, specs[chunk], traces, chunk, width, share
        )
        back = back.reshape(freq_devices, local, 2 * share, width)
        back = lax.all_to_all(back, "freq", split_axis=0, concat_axis=0, tiled=True)
        gathered.append(gather(back, groups))
    panel = None
    for chunk in range(chunks):
        panel = adjoint(me, refl, *gathered[chunk], panel, chunk, width, groups, share)
    panel = lax.all_to_all(panel, "freq", split_axis=0, concat_axis=0, tiled=True)
    panel = panel.reshape(freqs, groups // freq_devices * 2 * share, receivers)
    return traces, final(to_time, mute_receiver, panel, direct_wave, share)


def solution(mesh):
    placed = (
        P("freq", None, None, "rcv"),
        P("freq", None, None, "rcv"),
        P(None, "freq", "rcv"),
        P("rcv", "freq"),
        P("freq", "rcv"),
    )
    return jax.shard_map(
        body,
        mesh=mesh,
        in_specs=placed,
        out_specs=(P(None, "rcv", "freq"), P(None, "freq", "rcv")),
        check_vma=False,
    )
```
